512 devices in a mesh: row: 32 (over y, z_hi), col: 4 (over x), pair: 4 (over z_lo, core).
Axes of the slice: x: 4, y: 8, z: 8 (z_hi: 4, z_lo: 2; z = z_hi * 2 + z_lo), core: 2. Of those that a mesh axis runs over, the one named last changes fastest.
Arguments:
- amps: bfloat16 [512, 512, 512], P('pair', 'row', 'col'), may hold values from -6 to 6
- integrals: bfloat16 [4096, 512, 512], P('pair', 'row', 'col'), may hold values from -0.01171875 to 0.01171875
- mask_amps: int32 [8, 8], replicated, may hold values 0 or 1
- mask_ints: int32 [8, 8], replicated, may hold values 0 or 1
Outputs:
- residual: bfloat16 [512, 4096], P(('row', 'col'), 'pair')
The draws below stay inside these ranges and needn't reach their ends.
All inputs are finite; a program needn't handle non-finite values.
Results may differ from the reference program's by a relative error of at most 0.00115.
Values may be sent and summed in bfloat16 or wider, within the bound.
A program may use at most 64 MiB of HBM per device.

```python
import jax
import jax.numpy as jnp
from jax import lax

NV = 512
TILE = 64
WIN = 64
NPAIR = 512
NT = 8


def plant(array, stream_key, low, top_value):
    longest = array.shape.index(max(array.shape))
    spots = []
    for shift in (0, 1):
        where = [jax.random.randint(jax.random.fold_in(stream_key, axis), (), 0, length) for axis, length in enumerate(array.shape)]
        where[longest] = (where[longest] + shift) % array.shape[longest]
        spots.append(tuple(where))
    return array.at[spots[0]].set(low).at[spots[1]].set(top_value)


def spiked(entries, own_key, source, target, blocks, factor):
    owner, partner = [(jnp.arange(entries.shape[dim]) // (entries.shape[dim] // blocks)).reshape([-1 if axis == dim else 1 for axis in range(entries.ndim)]) for dim in (source, target)]
    chosen = jax.random.permutation(own_key, blocks)[partner]
    strong = (owner == chosen) | (owner == (partner + blocks // 2) % blocks)
    return jnp.where(strong, factor * entries, entries)


def block_scale(key, shape, cuts, smallest, largest):
    factor_of = 1.0
    for position, parts in cuts:
        draws = jax.random.uniform(jax.random.fold_in(jax.random.fold_in(key, 6), position), (parts,), jnp.float32, smallest / len(cuts), largest / len(cuts))
        factor_of = factor_of * jnp.repeat(jnp.exp(draws), shape[position] // parts).reshape((-1,) + (1,) * (len(shape) - 1 - position))
    return factor_of


def scatter_about(own_key, shape, scale, limit, shards=(), kind=jnp.bfloat16):
    array = scale * jax.random.normal(own_key, shape, jnp.float32)
    if shards:
        array = array * block_scale(own_key, shape, shards, -0.22, 0.18)
    return jnp.clip(array, -limit, limit).astype(kind)


def heavy_noise(key, dims, width, reach, cuts, heavy, dtype=jnp.bfloat16):
    drawn = width * jax.random.normal(key, dims, jnp.float32)
    if cuts:
        drawn = drawn * block_scale(key, dims, cuts, -0.22, 0.18)
    return jnp.clip(spiked(drawn, jax.random.fold_in(key, 3), *heavy), -reach, reach).astype(dtype)


def setup_inputs(seed: int = 0) -> dict:
    splits = jax.random.split(jax.random.key(seed), 5)
    return {
        "amps": heavy_noise(splits[0], (NPAIR, NV, NV), 1.0, 6.0, ((0, 4), (1, 32), (2, 4)), (1, 0, 32, 2.75)),
        "integrals": scatter_about(splits[1], (WIN * WIN, NV, NV), (NV * NV) ** -0.5, 0.01171875, ((0, 4), (1, 32), (2, 4))),
        "mask_amps": plant((jax.random.randint(splits[2], (NT, NT), 0, 4) < 3).astype(jnp.int32), jax.random.fold_in(splits[2], 1), 0, 1),
        "mask_ints": plant((jax.random.randint(splits[3], (NT, NT), 0, 4) < 3).astype(jnp.int32), jax.random.fold_in(splits[3], 1), 0, 1),
    }


def tile_factor(mask):
    tiles = jnp.arange(NV) // TILE
    onehot = (tiles[:, None] == jnp.arange(NT)[None, :]).astype(jnp.float32)
    return jnp.dot(jnp.dot(onehot, mask.astype(jnp.float32)), onehot.T)


def reference(amps, integrals, mask_amps, mask_ints):
    factor_amps = tile_factor(mask_amps).astype(jnp.bfloat16)
    factor_ints = tile_factor(mask_ints).astype(jnp.bfloat16)
    flat_amps = (amps * factor_amps[None]).reshape(NPAIR, NV * NV)
    grouped = integrals.reshape(WIN, WIN, NV, NV)

    def one_row(block):
        masked = (block * factor_ints[None]).reshape(WIN, NV * NV)
        return lax.dot_general(flat_amps, masked, (((1,), (1,)), ((), ())), preferred_element_type=jnp.float32)

    ladder = lax.map(one_row, grouped)
    ladder = jnp.transpose(ladder, (1, 0, 2))
    result = 0.5 * (ladder - jnp.transpose(ladder, (0, 2, 1)))
    return result.reshape(NPAIR, WIN * WIN).astype(jnp.bfloat16)
```

```python
import functools

import jax
import jax.numpy as jnp
from jax import lax
from jax.experimental import pallas as pl
from jax.experimental.pallas import tpu as pltpu
from jax.sharding import PartitionSpec as P

MESH = pl.DeviceIdType.MESH
NT_DIMS = (((1,), (1,)), ((), ()))
COLS = 768
PACKED = 512


def pack(v):
    top = jnp.maximum(jnp.max(jnp.abs(v), axis=1, keepdims=True), 1e-30)
    power = jnp.floor(jnp.log2(top)) + 1.0
    q = jnp.round(v * (jnp.exp2(15.0 - power) * 0.9999))
    q1, q2, q3 = q[:, 0:256], q[:, 256:512], q[:, 512:768]
    lane = lax.broadcasted_iota(jnp.int32, q3.shape, 1)
    q3 = jnp.where(lane == 120, power, q3)
    high = jnp.round(q3 * (1.0 / 256.0))
    low = q3 - 256.0 * high
    return jnp.concatenate([q1 * 512.0 + high, q2 * 512.0 + low], axis=1)


def unpack(w):
    w1, w2 = w[:, 0:256], w[:, 256:512]
    q1 = jnp.round(w1 * (1.0 / 512.0))
    q2 = jnp.round(w2 * (1.0 / 512.0))
    q3 = 256.0 * (w1 - 512.0 * q1) + (w2 - 512.0 * q2)
    power = q3[:, 120:121]
    scale = jnp.exp2(power - 15.0) * (1.0 / 0.9999)
    return jnp.concatenate([q1, q2, q3], axis=1) * scale


def store_group(slabs, dst, row):
    turned = jnp.swapaxes(slabs, 0, 1)
    for c in range(16):
        dst[pl.ds(row, 16), c * 128 : (c + 1) * 128] = turned[c]


def kernel(
    amps, ints, mask_a, mask_i, out,
    raw, ints_v, rcore, flat_a, flat_i, part, xsend, xrecv, ysend, yrecv, yown,
    zs, zsame, znbr, zq, place,
    lsem, asend, arecv, isend, irecv, xss, xrs, yss, yrs, zss, zrs,
):
    row, x, pair = lax.axis_index("row"), lax.axis_index("col"), lax.axis_index("pair")
    y, zh = row // 4, row % 4
    zl, c = pair // 2, pair % 2
    pn = 2 * zl + 1 - c

    def dev(y_=None, zh_=None, x_=None, pair_=None):
        yy = y if y_ is None else y_
        zz = zh if zh_ is None else zh_
        return {
            "row": yy * 4 + zz,
            "col": x if x_ is None else x_,
            "pair": pair if pair_ is None else pair_,
        }

    core_dev = dev(pair_=pn)
    zl_dev = dev(pair_=2 * (1 - zl) + c)

    def remote(src, dst, ss, rs, device):
        return pltpu.make_async_remote_copy(src, dst, ss, rs, device_id=device, device_id_type=MESH)

    barrier = pltpu.get_barrier_semaphore()
    peers = [dev(x_=(x + j) % 4) for j in range(1, 4)]
    peers += [dev(y_=(y + j) % 8) for j in range(1, 8)]
    peers += [
        dev(zh_=(zh + jz) % 4, pair_=(pair + jp) % 4) for jz in range(4) for jp in range(4) if jz or jp
    ]
    for device in peers:
        pl.semaphore_signal(barrier, inc=1, device_id=device, device_id_type=MESH)

    own_copy = pltpu.make_async_copy(amps, raw.at[0], lsem.at[0])
    own_copy.start()
    ints_copy = pltpu.make_async_copy(ints, ints_v, lsem.at[1])
    ints_copy.start()
    pl.semaphore_wait(barrier, len(peers))

    sends = []
    core_amps = remote(amps, raw.at[1], asend.at[0], arecv.at[0], core_dev)
    core_amps.start()
    sends.append(core_amps)
    zcopies = []
    for k in range(4):
        cp = remote(amps.at[pl.ds(32 * k, 32)], raw.at[2, pl.ds(32 * k, 32)], asend.at[1 + k], arecv.at[1 + k], zl_dev)
        cp.start()
        zcopies.append(cp)
        sends.append(cp)
    icopies = []
    for a in range(2):
        vh = (a + 1 + c) % 2
        cp = remote(
            ints.at[pl.ds(8 * a, 8), pl.ds(16 * pn + 8 * vh, 8)], rcore.at[a], isend.at[a], irecv.at[a], core_dev
        )
        cp.start()
        icopies.append(cp)
        sends.append(cp)

    m0 = (mask_a[y, 2 * x] * mask_i[y, 2 * x]).astype(jnp.float32)
    m1 = (mask_a[y, 2 * x + 1] * mask_i[y, 2 * x + 1]).astype(jnp.float32)
    lane = lax.broadcasted_iota(jnp.int32, (16, 128), 1)
    factor = jnp.where(lane < 64, m0, m1).astype(jnp.bfloat16)

    def amps_rows(first, second, k, xq, dst_row):
        parts = [
            raw[src, pl.ds(32 * k + 16 * zb + 4 * xq, 4)] for src in (first, second) for zb in range(2)
        ]
        store_group(jnp.concatenate(parts, axis=0) * factor[None], flat_a, dst_row)

    def ints_rows(slabs, dst_row):
        store_group(jnp.concatenate([ints_v[a, pl.ds(b, 1)] for a, b in slabs], axis=0), flat_i, dst_row)

    own_copy.wait()
    ints_copy.wait()

    def cross(g, _):
        for j in range(2):
            q = 2 * (1 - zl) + j
            slabs = [((1 - zl) * g + zl * r, 16 * q + (1 - zl) * r + zl * g) for r in range(16)]
            ints_rows(slabs, pl.multiple_of(256 * j + 16 * g, 16))
        return 0

    lax.fori_loop(0, 16, cross, 0)

    def diagonal(g, _):
        turn = [(r + g + 1) % 16 for r in range(16)]
        ints_rows([(r, 16 * pair + turn[r]) for r in range(16)], pl.multiple_of(512 + 16 * g, 16))
        ints_rows([(turn[r], 16 * pair + r) for r in range(16)], pl.multiple_of(768 + 16 * g, 16))
        half = g // 4
        vh = (half + c) % 2
        slabs = [(8 * half + 2 * (g % 4) + r // 8, 16 * pn + 8 * vh + r % 8) for r in range(16)]
        ints_rows(slabs, pl.multiple_of(640 + 16 * g, 16))
        return 0

    lax.fori_loop(0, 8, diagonal, 0)
    for cp in icopies:
        cp.wait_recv()

    def minus(g, _):
        half = (g // 4 + c) % 2
        slabs = [rcore[half, r % 8, pl.ds(2 * (g % 4) + r // 8, 1)] for r in range(16)]
        store_group(jnp.concatenate(slabs, axis=0), flat_i, pl.multiple_of(896 + 16 * g, 16))
        return 0

    lax.fori_loop(0, 8, minus, 0)
    core_amps.wait_recv()

    def early_rows(n, _):
        amps_rows(0, 1, n // 4, n % 4, pl.multiple_of(16 * n, 16))
        return 0

    lax.fori_loop(0, 16, early_rows, 0)

    def ladder(row0, rows):
        a = flat_a[row0 : row0 + rows, :]
        for n in range(2):
            part[row0 : row0 + rows, 256 * n : 256 * (n + 1)] = lax.dot_general(
                a, flat_i[256 * n : 256 * (n + 1), :], NT_DIMS, preferred_element_type=jnp.float32
            )
        plus = lax.dot_general(a, flat_i[512:768, :], NT_DIMS, preferred_element_type=jnp.float32)
        less = lax.dot_general(a, flat_i[768:1024, :], NT_DIMS, preferred_element_type=jnp.float32)
        part[row0 : row0 + rows, 512:768] = plus - less

    def xcopy(s, j):
        to = (x + j) % 4
        return remote(
            xsend.at[s, to], xrecv.at[s, j - 1], xss.at[s, j - 1], xrs.at[s, j - 1], dev(x_=to)
        )

    def send_x(s):
        packed = pack(part[64 * s : 64 * s + 64, :])
        for xq in range(4):
            xsend[s, xq] = packed[16 * xq : 16 * xq + 16]
        for j in (2, 1, 3):
            xcopy(s, j).start()

    def ydest(s, slot):
        k = s % 4
        zsrc = zl if s < 4 else 1 - zl
        p = 2 * zsrc + (c if slot == 0 else 1 - c)
        to = 2 * p + k // 2
        return to, (y - to + 8) % 8, k % 2

    def ycopy(s, slot):
        to, j, h = ydest(s, slot)
        return remote(ysend.at[s, slot], yrecv.at[h, j], yss.at[s, slot], yrs.at[h, j], dev(y_=to))

    def reduce_x(s):
        for j in (1, 3, 2):
            xcopy(s, j).wait_recv()
        total = part[pl.ds(pl.multiple_of(64 * s + 16 * x, 16), 16), :]
        for j in (1, 3, 2):
            total = total + unpack(xrecv[s, j - 1])
        packed = pack(total)
        for slot in range(2):
            ysend[s, slot] = packed[8 * slot : 8 * slot + 8]
            _, j, h = ydest(s, slot)

            @pl.when(j != 0)
            def _():
                ycopy(s, slot).start()

            @pl.when(j == 0)
            def _():
                yown[h] = total[8 * slot : 8 * slot + 8]

    ladder(0, 256)
    for s in range(4):
        send_x(s)

    def build_place():
        col = lax.broadcasted_iota(jnp.int32, (1, 1024), 1)
        u, b = col // 64, col % 64
        block, v = b // 16, b % 16
        turn = (v - u + 16) % 16
        diag_plus = jnp.logical_or(turn < 8, jnp.logical_and(turn == 8, u < 8))
        src = jnp.where(diag_plus, 512 + (turn - 1) * 16 + u, 512 + (15 - turn) * 16 + v)
        sign = jnp.where(diag_plus, 1.0, -1.0)
        src = jnp.where(turn == 0, -1, src)
        uh, vh, u8, v8 = u // 8, v // 8, u % 8, v % 8
        mine = (uh + vh) % 2 == c
        near = block == pn
        src = jnp.where(near, jnp.where(mine, 640 + uh * 64 + u8 * 8 + v8, 768 + vh * 64 + v8 * 8 + u8), src)
        sign = jnp.where(near, jnp.where(mine, 1.0, -1.0), sign)
        far = block // 2 == 1 - zl
        src = jnp.where(far, (block % 2) * 256 + (1 - zl) * (u * 16 + v) + zl * (v * 16 + u), src)
        sign = jnp.where(far, 1.0, sign)

        def body(r, _):
            rows = r * 64 + lax.broadcasted_iota(jnp.int32, (64, 1024), 0)
            picked = jnp.where(rows == src, sign, 0.0)
            place[pl.ds(pl.multiple_of(r * 64, 64), 64), :] = picked.astype(jnp.bfloat16)
            return 0

        lax.fori_loop(0, 14, body, 0)

    build_place()

    fwds = []
    for k in range(4):
        s = 4 + k
        zcopies[k].wait_recv()
        fwd = remote(
            raw.at[2, pl.ds(32 * k, 32)], raw.at[3, pl.ds(32 * k, 32)], asend.at[5 + k], arecv.at[5 + k], core_dev
        )
        fwd.start()
        fwds.append(fwd)
        if k == 1:
            reduce_x(0)
        if k == 2:
            reduce_x(1)
        if k == 3:
            reduce_x(2)
            reduce_x(3)
        fwd.wait_recv()

        def late_rows(n, _):
            amps_rows(2, 3, k, n, pl.multiple_of(64 * s + 16 * n, 16))
            return 0

        lax.fori_loop(0, 4, late_rows, 0)
        ladder(64 * s, 64)
        send_x(s)
    for s in range(4, 8):
        reduce_x(s)

    for h in range(2):
        total = yown[h]
        for j in range(1, 8):
            remote(ysend.at[0, 0], yrecv.at[h, j], yss.at[0, 0], yrs.at[h, j], core_dev).wait_recv()
            total = total + unpack(yrecv[h, j])
        for zb in range(2):
            zs[2 * h + zb] = total[4 * zb : 4 * zb + 4]

    zcps = []
    for jz in (2, 1, 3, 0):
        to = (zh + jz) % 4
        for j in range(2):
            zcps.append(
                remote(
                    zs.at[to, :, pl.ds(256 * j, 256)], zq.at[c, jz], zss.at[jz, j], zrs.at[jz, c],
                    dev(zh_=to, pair_=2 * (1 - zl) + j),
                )
            )
        if jz:
            zcps.append(remote(zs.at[to], zsame.at[jz - 1], zss.at[jz, 2], zrs.at[jz, 2], dev(zh_=to)))
        zcps.append(
            remote(zs.at[to, :, pl.ds(640, 128)], znbr.at[jz], zss.at[jz, 3], zrs.at[jz, 3], dev(zh_=to, pair_=pn))
        )
    for cp in zcps:
        cp.start()

    for cp in sends + fwds:
        cp.wait_send()
    for s in range(8):
        for j in range(1, 4):
            xcopy(s, j).wait_send()
        for slot in range(2):
            @pl.when(ydest(s, slot)[1] != 0)
            def _():
                ycopy(s, slot).wait_send()

    same = zs[zh]
    for jz in range(1, 4):
        remote(zs.at[0], zsame.at[jz - 1], zss.at[jz, 2], zrs.at[jz, 2], core_dev).wait_recv()
        same = same + zsame[jz - 1]
    near = None
    for jz in range(4):
        remote(zs.at[0, :, pl.ds(0, 128)], znbr.at[jz], zss.at[jz, 3], zrs.at[jz, 3], core_dev).wait_recv()
        near = znbr[jz] if near is None else near + znbr[jz]
    far = []
    for j in range(2):
        got = None
        for jz in range(4):
            remote(zs.at[0, :, pl.ds(0, 256)], zq.at[j, jz], zss.at[jz, j], zrs.at[jz, j], core_dev).wait_recv()
            got = zq[j, jz] if got is None else got + zq[j, jz]
        far.append(got)
    values = jnp.concatenate(
        [same[:, 0:256] - far[0], same[:, 256:512] - far[1], same[:, 512:768], near], axis=1
    )
    values = (0.5 * values).astype(jnp.bfloat16)
    out[...] = jnp.dot(values, place[...], preferred_element_type=jnp.float32).astype(jnp.bfloat16)
    for cp in zcps:
        cp.wait_send()


def per_device(amps, integrals, mask_amps, mask_ints):
    ints = integrals.reshape(16, 64, 16, 128)
    bf, f32 = jnp.bfloat16, jnp.float32
    dma = pltpu.SemaphoreType.DMA
    return pl.pallas_call(
        kernel,
        out_shape=jax.ShapeDtypeStruct((4, 1024), bf),
        in_specs=[pl.BlockSpec(memory_space=pl.ANY)] * 2 + [pl.BlockSpec(memory_space=pltpu.SMEM)] * 2,
        out_specs=pl.BlockSpec(memory_space=pltpu.VMEM),
        scratch_shapes=[
            pltpu.VMEM((4, 128, 16, 128), bf),
            pltpu.VMEM((16, 64, 16, 128), bf),
            pltpu.VMEM((2, 8, 8, 16, 128), bf),
            pltpu.VMEM((512, 2048), bf),
            pltpu.VMEM((1024, 2048), bf),
            pltpu.VMEM((512, COLS), f32),
            pltpu.VMEM((8, 4, 16, PACKED), f32),
            pltpu.VMEM((8, 3, 16, PACKED), f32),
            pltpu.VMEM((8, 2, 8, PACKED), f32),
            pltpu.VMEM((2, 8, 8, PACKED), f32),
            pltpu.VMEM((2, 8, COLS), f32),
            pltpu.VMEM((4, 4, COLS), f32),
            pltpu.VMEM((3, 4, COLS), f32),
            pltpu.VMEM((4, 4, 128), f32),
            pltpu.VMEM((2, 4, 4, 256), f32),
            pltpu.VMEM((896, 1024), bf),
            dma((2,)), dma((9,)), dma((9,)), dma((2,)), dma((2,)),
            dma((8, 3)), dma((8, 3)), dma((8, 2)), dma((2, 8)), dma((4, 4)), dma((4, 4)),
        ],
        compiler_params=pltpu.CompilerParams(
            collective_id=0, has_side_effects=True, vmem_limit_bytes=48 * 2**20
        ),
        cost_estimate=pl.CostEstimate(flops=2 * 512 * 1024 * 2048, bytes_accessed=5 * 2**20, transcendentals=0),
    )(amps, ints, mask_amps, mask_ints)


def solution(mesh):
    return jax.shard_map(
        per_device,
        mesh=mesh,
        in_specs=(P("pair", "row", "col"), P("pair", "row", "col"), P(), P()),
        out_specs=P(("row", "col"), "pair"),
        check_vma=False,
    )
```

```python
import functools

import jax
import jax.numpy as jnp
from jax import lax
from jax.experimental import pallas as pl
from jax.experimental.pallas import tpu as pltpu
from jax.sharding import PartitionSpec as P

MESH = pl.DeviceIdType.MESH
NT_DIMS = (((1,), (1,)), ((), ()))
COLS = 768
PACKED = 512


def pack(v):
    top = jnp.maximum(jnp.max(jnp.abs(v), axis=1, keepdims=True), 1e-30)
    power = jnp.floor(jnp.log2(top)) + 1.0
    q = jnp.round(v * (jnp.exp2(15.0 - power) * 0.9999))
    q1, q2, q3 = q[:, 0:256], q[:, 256:512], q[:, 512:768]
    lane = lax.broadcasted_iota(jnp.int32, q3.shape, 1)
    q3 = jnp.where(lane == 120, power, q3)
    high = jnp.round(q3 * (1.0 / 256.0))
    low = q3 - 256.0 * high
    return jnp.concatenate([q1 * 512.0 + high, q2 * 512.0 + low], axis=1)


def unpack(w):
    w1, w2 = w[:, 0:256], w[:, 256:512]
    q1 = jnp.round(w1 * (1.0 / 512.0))
    q2 = jnp.round(w2 * (1.0 / 512.0))
    q3 = 256.0 * (w1 - 512.0 * q1) + (w2 - 512.0 * q2)
    power = q3[:, 120:121]
    scale = jnp.exp2(power - 15.0) * (1.0 / 0.9999)
    return jnp.concatenate([q1, q2, q3], axis=1) * scale


def store_group(slabs, dst, row):
    turned = jnp.swapaxes(slabs, 0, 1)
    for c in range(16):
        dst[pl.ds(row, 16), c * 128 : (c + 1) * 128] = turned[c]


def kernel(
    amps, ints, mask_a_hbm, mask_i_hbm, out,
    mask_a, mask_i, raw, ints_v, rcore, flat_a, flat_i, part, xsend, xrecv, ysend, yrecv, yown,
    zs, zsame, znbr, zq, place,
    lsem, asend, arecv, isend, irecv, xss, xrs, yss, yrs, zss, zrs,
):
    row, x, pair = lax.axis_index("row"), lax.axis_index("col"), lax.axis_index("pair")
    y, zh = row // 4, row % 4
    zl, c = pair // 2, pair % 2
    pn = 2 * zl + 1 - c

    def dev(y_=None, zh_=None, x_=None, pair_=None):
        yy = y if y_ is None else y_
        zz = zh if zh_ is None else zh_
        return {
            "row": yy * 4 + zz,
            "col": x if x_ is None else x_,
            "pair": pair if pair_ is None else pair_,
        }

    core_dev = dev(pair_=pn)
    zl_dev = dev(pair_=2 * (1 - zl) + c)

    def first_row(k, zb):
        return 64 * (k // 2) + 32 * zb + 16 * (k % 2)

    def remote(src, dst, ss, rs, device):
        return pltpu.make_async_remote_copy(src, dst, ss, rs, device_id=device, device_id_type=MESH)

    barrier = pltpu.get_barrier_semaphore()
    peers = [dev(x_=(x + j) % 4) for j in range(1, 4)]
    peers += [dev(y_=(y + j) % 8) for j in range(1, 8)]
    peers += [
        dev(zh_=(zh + jz) % 4, pair_=(pair + jp) % 4) for jz in range(4) for jp in range(4) if jz or jp
    ]
    for device in peers:
        pl.semaphore_signal(barrier, inc=1, device_id=device, device_id_type=MESH)

    own_copy = pltpu.make_async_copy(amps, raw.at[0], lsem.at[0])
    own_copy.start()
    ints_copy = pltpu.make_async_copy(ints, ints_v, lsem.at[1])
    ints_copy.start()
    mask_copies = [
        pltpu.make_async_copy(mask_a_hbm, mask_a, lsem.at[2]),
        pltpu.make_async_copy(mask_i_hbm, mask_i, lsem.at[3]),
    ]
    for cp in mask_copies:
        cp.start()
    pl.semaphore_wait(barrier, len(peers))

    sends = []
    core_amps = remote(amps, raw.at[1], asend.at[0], arecv.at[0], core_dev)
    core_amps.start()
    sends.append(core_amps)
    zcopies = []
    for n in range(8):
        at = pl.ds(first_row(n // 2, n % 2), 16)
        cp = remote(amps.at[at], raw.at[2, at], asend.at[1 + n], arecv.at[1 + n], zl_dev)
        cp.start()
        zcopies.append(cp)
        sends.append(cp)
    icopies = []
    for a in range(2):
        vh = (a + 1 + c) % 2
        cp = remote(
            ints.at[pl.ds(8 * a, 8), pl.ds(16 * pn + 8 * vh, 8)], rcore.at[a], isend.at[a], irecv.at[a], core_dev
        )
        cp.start()
        icopies.append(cp)
        sends.append(cp)

    for cp in mask_copies:
        cp.wait()
    m0 = (mask_a[y, 2 * x] * mask_i[y, 2 * x]).astype(jnp.float32)
    m1 = (mask_a[y, 2 * x + 1] * mask_i[y, 2 * x + 1]).astype(jnp.float32)
    lane = lax.broadcasted_iota(jnp.int32, (16, 128), 1)
    factor = jnp.where(lane < 64, m0, m1).astype(jnp.bfloat16)

    def amps_rows(first, second, k, xq, dst_row):
        parts = [
            raw[src, pl.ds(first_row(k, zb) + 4 * xq, 4)] for src in (first, second) for zb in range(2)
        ]
        store_group(jnp.concatenate(parts, axis=0) * factor[None], flat_a, dst_row)

    def ints_rows(slabs, dst_row):
        store_group(jnp.concatenate([ints_v[a, pl.ds(b, 1)] for a, b in slabs], axis=0), flat_i, dst_row)

    own_copy.wait()
    ints_copy.wait()

    def cross(g, _):
        for j in range(2):
            q = 2 * (1 - zl) + j
            slabs = [((1 - zl) * g + zl * r, 16 * q + (1 - zl) * r + zl * g) for r in range(16)]
            ints_rows(slabs, pl.multiple_of(256 * j + 16 * g, 16))
        return 0

    lax.fori_loop(0, 16, cross, 0)

    def diagonal(g, _):
        turn = [(r + g + 1) % 16 for r in range(16)]
        ints_rows([(r, 16 * pair + turn[r]) for r in range(16)], pl.multiple_of(512 + 16 * g, 16))
        ints_rows([(turn[r], 16 * pair + r) for r in range(16)], pl.multiple_of(768 + 16 * g, 16))
        half = g // 4
        vh = (half + c) % 2
        slabs = [(8 * half + 2 * (g % 4) + r // 8, 16 * pn + 8 * vh + r % 8) for r in range(16)]
        ints_rows(slabs, pl.multiple_of(640 + 16 * g, 16))
        return 0

    lax.fori_loop(0, 8, diagonal, 0)
    for cp in icopies:
        cp.wait_recv()

    def minus(g, _):
        half = (g // 4 + c) % 2
        slabs = [rcore[half, r % 8, pl.ds(2 * (g % 4) + r // 8, 1)] for r in range(16)]
        store_group(jnp.concatenate(slabs, axis=0), flat_i, pl.multiple_of(896 + 16 * g, 16))
        return 0

    lax.fori_loop(0, 8, minus, 0)
    core_amps.wait_recv()

    def early_rows(n, _):
        amps_rows(0, 1, n // 4, n % 4, pl.multiple_of(16 * n, 16))
        return 0

    lax.fori_loop(0, 16, early_rows, 0)

    def ladder(row0, rows):
        a = flat_a[row0 : row0 + rows, :]
        for n in range(2):
            part[row0 : row0 + rows, 256 * n : 256 * (n + 1)] = lax.dot_general(
                a, flat_i[256 * n : 256 * (n + 1), :], NT_DIMS, preferred_element_type=jnp.float32
            )
        plus = lax.dot_general(a, flat_i[512:768, :], NT_DIMS, preferred_element_type=jnp.float32)
        less = lax.dot_general(a, flat_i[768:1024, :], NT_DIMS, preferred_element_type=jnp.float32)
        part[row0 : row0 + rows, 512:768] = plus - less

    def xcopy(s, j):
        to = (x + j) % 4
        return remote(
            xsend.at[s, to], xrecv.at[s, j - 1], xss.at[s, j - 1], xrs.at[s, j - 1], dev(x_=to)
        )

    def send_x(s):
        packed = pack(part[64 * s : 64 * s + 64, :])
        for xq in range(4):
            xsend[s, xq] = packed[16 * xq : 16 * xq + 16]
        for j in (2, 1, 3):
            xcopy(s, j).start()

    def ydest(s, slot):
        k = s % 4
        zsrc = zl if s < 4 else 1 - zl
        p = 2 * zsrc + (c if slot == 0 else 1 - c)
        to = 2 * p + k // 2
        return to, (y - to + 8) % 8, k % 2

    def ycopy(s, slot):
        to, j, h = ydest(s, slot)
        return remote(ysend.at[s, slot], yrecv.at[h, j], yss.at[s, slot], yrs.at[h, j], dev(y_=to))

    def reduce_x(s):
        for j in (1, 3, 2):
            xcopy(s, j).wait_recv()
        total = part[pl.ds(pl.multiple_of(64 * s + 16 * x, 16), 16), :]
        for j in (1, 3, 2):
            total = total + unpack(xrecv[s, j - 1])
        packed = pack(total)
        for slot in range(2):
            ysend[s, slot] = packed[8 * slot : 8 * slot + 8]
            _, j, h = ydest(s, slot)

            @pl.when(j != 0)
            def _():
                ycopy(s, slot).start()

            @pl.when(j == 0)
            def _():
                yown[h] = total[8 * slot : 8 * slot + 8]

    ladder(0, 256)
    for s in range(4):
        send_x(s)

    def build_place():
        col = lax.broadcasted_iota(jnp.int32, (1, 1024), 1)
        u, b = col // 64, col % 64
        block, v = b // 16, b % 16
        turn = (v - u + 16) % 16
        diag_plus = jnp.logical_or(turn < 8, jnp.logical_and(turn == 8, u < 8))
        src = jnp.where(diag_plus, 512 + (turn - 1) * 16 + u, 512 + (15 - turn) * 16 + v)
        sign = jnp.where(diag_plus, 1.0, -1.0)
        src = jnp.where(turn == 0, -1, src)
        uh, vh, u8, v8 = u // 8, v // 8, u % 8, v % 8
        mine = (uh + vh) % 2 == c
        near = block == pn
        src = jnp.where(near, jnp.where(mine, 640 + uh * 64 + u8 * 8 + v8, 768 + vh * 64 + v8 * 8 + u8), src)
        sign = jnp.where(near, jnp.where(mine, 1.0, -1.0), sign)
        far = block // 2 == 1 - zl
        src = jnp.where(far, (block % 2) * 256 + (1 - zl) * (u * 16 + v) + zl * (v * 16 + u), src)
        sign = jnp.where(far, 1.0, sign)

        def body(r, _):
            rows = r * 64 + lax.broadcasted_iota(jnp.int32, (64, 1024), 0)
            picked = jnp.where(rows == src, sign, 0.0)
            place[pl.ds(pl.multiple_of(r * 64, 64), 64), :] = picked.astype(jnp.bfloat16)
            return 0

        lax.fori_loop(0, 14, body, 0)

    build_place()

    fwds = []
    for k in range(4):
        s = 4 + k
        for n in (2 * k, 2 * k + 1):
            zcopies[n].wait_recv()
            at = pl.ds(first_row(k, n % 2), 16)
            fwd = remote(raw.at[2, at], raw.at[3, at], asend.at[9 + n], arecv.at[9 + n], core_dev)
            fwd.start()
            fwds.append(fwd)
        if k == 1:
            reduce_x(0)
        if k == 2:
            reduce_x(1)
        if k == 3:
            reduce_x(2)
            reduce_x(3)
        for fwd in fwds[2 * k :]:
            fwd.wait_recv()

        def late_rows(n, _):
            amps_rows(2, 3, k, n, pl.multiple_of(64 * s + 16 * n, 16))
            return 0

        lax.fori_loop(0, 4, late_rows, 0)
        ladder(64 * s, 64)
        send_x(s)
    for s in range(4, 8):
        reduce_x(s)

    def zcopies_of(to, n):
        jz = (to - zh + 4) % 4
        far = [
            remote(
                zs.at[to, :, pl.ds(256 * j, 256)], zq.at[c, jz], zss.at[n, j], zrs.at[jz, c],
                dev(zh_=to, pair_=2 * (1 - zl) + j),
            )
            for j in range(2)
        ]
        near = remote(
            zs.at[to, :, pl.ds(640, 128)], znbr.at[jz], zss.at[n, 3], zrs.at[jz, 3], dev(zh_=to, pair_=pn)
        )
        return jz, far + [near], remote(zs.at[to], zsame.at[jz], zss.at[n, 2], zrs.at[jz, 2], dev(zh_=to))

    for h in range(2):
        total = yown[h]
        for j in range(1, 8):
            remote(ysend.at[0, 0], yrecv.at[h, j], yss.at[0, 0], yrs.at[h, j], core_dev).wait_recv()
            total = total + unpack(yrecv[h, j])
        for zb in range(2):
            zs[2 * zb + h] = total[4 * zb : 4 * zb + 4]
        for zb in range(2):
            jz, copies, same_copy = zcopies_of(2 * zb + h, 2 * zb + h)

            @pl.when(jz != 0)
            def _():
                same_copy.start()

            for cp in copies:
                cp.start()

    for cp in sends + fwds:
        cp.wait_send()
    for s in range(8):
        for j in range(1, 4):
            xcopy(s, j).wait_send()
        for slot in range(2):
            @pl.when(ydest(s, slot)[1] != 0)
            def _():
                ycopy(s, slot).wait_send()

    same = zs[zh]
    for jz in range(1, 4):
        remote(zs.at[0], zsame.at[jz], zss.at[jz, 2], zrs.at[jz, 2], core_dev).wait_recv()
        same = same + zsame[jz]
    near = None
    for jz in range(4):
        remote(zs.at[0, :, pl.ds(0, 128)], znbr.at[jz], zss.at[jz, 3], zrs.at[jz, 3], core_dev).wait_recv()
        near = znbr[jz] if near is None else near + znbr[jz]
    far = []
    for j in range(2):
        got = None
        for jz in range(4):
            remote(zs.at[0, :, pl.ds(0, 256)], zq.at[j, jz], zss.at[jz, j], zrs.at[jz, j], core_dev).wait_recv()
            got = zq[j, jz] if got is None else got + zq[j, jz]
        far.append(got)
    values = jnp.concatenate(
        [same[:, 0:256] - far[0], same[:, 256:512] - far[1], same[:, 512:768], near], axis=1
    )
    values = (0.5 * values).astype(jnp.bfloat16)
    out[...] = jnp.dot(values, place[...], preferred_element_type=jnp.float32).astype(jnp.bfloat16)
    for n in range(4):
        jz, copies, same_copy = zcopies_of(n, n)
        for cp in copies:
            cp.wait_send()

        @pl.when(jz != 0)
        def _():
            same_copy.wait_send()


def per_device(amps, integrals, mask_amps, mask_ints):
    ints = integrals.reshape(16, 64, 16, 128)
    bf, f32 = jnp.bfloat16, jnp.float32
    dma = pltpu.SemaphoreType.DMA
    return pl.pallas_call(
        kernel,
        out_shape=jax.ShapeDtypeStruct((4, 1024), bf),
        in_specs=[pl.BlockSpec(memory_space=pltpu.HBM)] * 4,
        out_specs=pl.BlockSpec(memory_space=pltpu.VMEM),
        scratch_shapes=[
            pltpu.SMEM((8, 8), jnp.int32),
            pltpu.SMEM((8, 8), jnp.int32),
            pltpu.VMEM((4, 128, 16, 128), bf),
            pltpu.VMEM((16, 64, 16, 128), bf),
            pltpu.VMEM((2, 8, 8, 16, 128), bf),
            pltpu.VMEM((512, 2048), bf),
            pltpu.VMEM((1024, 2048), bf),
            pltpu.VMEM((512, COLS), f32),
            pltpu.VMEM((8, 4, 16, PACKED), f32),
            pltpu.VMEM((8, 3, 16, PACKED), f32),
            pltpu.VMEM((8, 2, 8, PACKED), f32),
            pltpu.VMEM((2, 8, 8, PACKED), f32),
            pltpu.VMEM((2, 8, COLS), f32),
            pltpu.VMEM((4, 4, COLS), f32),
            pltpu.VMEM((4, 4, COLS), f32),
            pltpu.VMEM((4, 4, 128), f32),
            pltpu.VMEM((2, 4, 4, 256), f32),
            pltpu.VMEM((896, 1024), bf),
            dma((4,)), dma((17,)), dma((17,)), dma((2,)), dma((2,)),
            dma((8, 3)), dma((8, 3)), dma((8, 2)), dma((2, 8)), dma((4, 4)), dma((4, 4)),
        ],
        compiler_params=pltpu.CompilerParams(
            collective_id=0, has_side_effects=True, vmem_limit_bytes=61 * 2**20
        ),
        cost_estimate=pl.CostEstimate(flops=2 * 512 * 1024 * 2048, bytes_accessed=5 * 2**20, transcendentals=0),
    )(amps, ints, mask_amps, mask_ints)


def solution(mesh):
    return jax.shard_map(
        per_device,
        mesh=mesh,
        in_specs=(P("pair", "row", "col"), P("pair", "row", "col"), P(), P()),
        out_specs=P(("row", "col"), "pair"),
        check_vma=False,
    )
```

```python
import functools

import jax
import jax.numpy as jnp
from jax import lax
from jax.experimental import pallas as pl
from jax.experimental.pallas import tpu as pltpu
from jax.sharding import PartitionSpec as P

MESH = pl.DeviceIdType.MESH
NT_DIMS = (((1,), (1,)), ((), ()))
COLS = 768
PACKED = 512


def pack(v):
    top = jnp.maximum(jnp.max(jnp.abs(v), axis=1, keepdims=True), 1e-30)
    power = jnp.floor(jnp.log2(top)) + 1.0
    q = jnp.round(v * (jnp.exp2(15.0 - power) * 0.9999))
    q1, q2, q3 = q[:, 0:256], q[:, 256:512], q[:, 512:768]
    lane = lax.broadcasted_iota(jnp.int32, q3.shape, 1)
    q3 = jnp.where(lane == 120, power, q3)
    high = jnp.round(q3 * (1.0 / 256.0))
    low = q3 - 256.0 * high
    return jnp.concatenate([q1 * 512.0 + high, q2 * 512.0 + low], axis=1)


def unpack(w):
    w1, w2 = w[:, 0:256], w[:, 256:512]
    q1 = jnp.round(w1 * (1.0 / 512.0))
    q2 = jnp.round(w2 * (1.0 / 512.0))
    q3 = 256.0 * (w1 - 512.0 * q1) + (w2 - 512.0 * q2)
    power = q3[:, 120:121]
    scale = jnp.exp2(power - 15.0) * (1.0 / 0.9999)
    return jnp.concatenate([q1, q2, q3], axis=1) * scale


def store_group(slabs, dst, row):
    turned = jnp.swapaxes(slabs, 0, 1)
    for c in range(16):
        dst[pl.ds(row, 16), c * 128 : (c + 1) * 128] = turned[c]


def kernel(
    amps, ints, mask_a_hbm, mask_i_hbm, out,
    mask_a, mask_i, raw, ints_v, rcore, flat_a, flat_i, flat_t, part, xsend, xrecv, ysend, yrecv, yown,
    zs, zsame, znbr, zq, place,
    lsem, asend, arecv, isend, irecv, xss, xrs, yss, yrs, zss, zrs,
):
    row, x, pair = lax.axis_index("row"), lax.axis_index("col"), lax.axis_index("pair")
    y, zh = row // 4, row % 4
    zl, c = pair // 2, pair % 2
    pn = 2 * zl + 1 - c

    def dev(y_=None, zh_=None, x_=None, pair_=None):
        yy = y if y_ is None else y_
        zz = zh if zh_ is None else zh_
        return {
            "row": yy * 4 + zz,
            "col": x if x_ is None else x_,
            "pair": pair if pair_ is None else pair_,
        }

    core_dev = dev(pair_=pn)
    zl_dev = dev(pair_=2 * (1 - zl) + c)

    def first_row(k, zb):
        return 64 * (k // 2) + 32 * zb + 16 * (k % 2)

    def remote(src, dst, ss, rs, device):
        return pltpu.make_async_remote_copy(src, dst, ss, rs, device_id=device, device_id_type=MESH)

    barrier = pltpu.get_barrier_semaphore()
    peers = [dev(x_=(x + j) % 4) for j in range(1, 4)]
    peers += [dev(y_=(y + j) % 8) for j in range(1, 8)]
    peers += [
        dev(zh_=(zh + jz) % 4, pair_=(pair + jp) % 4) for jz in range(4) for jp in range(4) if jz or jp
    ]
    for device in peers:
        pl.semaphore_signal(barrier, inc=1, device_id=device, device_id_type=MESH)

    own_copy = pltpu.make_async_copy(amps, raw.at[0], lsem.at[0])
    own_copy.start()
    ints_copy = pltpu.make_async_copy(ints, ints_v, lsem.at[1])
    ints_copy.start()
    mask_copies = [
        pltpu.make_async_copy(mask_a_hbm, mask_a, lsem.at[2]),
        pltpu.make_async_copy(mask_i_hbm, mask_i, lsem.at[3]),
    ]
    for cp in mask_copies:
        cp.start()
    pl.semaphore_wait(barrier, len(peers))

    sends = []
    core_amps = remote(amps, raw.at[1], asend.at[0], arecv.at[0], core_dev)
    core_amps.start()
    sends.append(core_amps)
    zcopies = []
    for n in range(8):
        at = pl.ds(first_row(n // 2, n % 2), 16)
        cp = remote(amps.at[at], raw.at[2, at], asend.at[1 + n], arecv.at[1 + n], zl_dev)
        cp.start()
        zcopies.append(cp)
        sends.append(cp)
    icopies = []
    for a in range(2):
        vh = (a + 1 + c) % 2
        cp = remote(
            ints.at[pl.ds(8 * a, 8), pl.ds(16 * pn + 8 * vh, 8)], rcore.at[a], isend.at[a], irecv.at[a], core_dev
        )
        cp.start()
        icopies.append(cp)
        sends.append(cp)

    for cp in mask_copies:
        cp.wait()
    m0 = (mask_a[y, 2 * x] * mask_i[y, 2 * x]).astype(jnp.float32)
    m1 = (mask_a[y, 2 * x + 1] * mask_i[y, 2 * x + 1]).astype(jnp.float32)
    lane = lax.broadcasted_iota(jnp.int32, (16, 128), 1)
    factor = jnp.where(lane < 64, m0, m1).astype(jnp.bfloat16)

    def amps_rows(first, second, k, xq, dst_row):
        parts = [
            raw[src, pl.ds(first_row(k, zb) + 4 * xq, 4)] for src in (first, second) for zb in range(2)
        ]
        store_group(jnp.concatenate(parts, axis=0) * factor[None], flat_a, dst_row)

    def ints_rows(slabs, dst_row):
        store_group(jnp.concatenate([ints_v[a, pl.ds(b, 1)] for a, b in slabs], axis=0), flat_i, dst_row)

    own_copy.wait()
    ints_copy.wait()

    def cross(g, _):
        for j in range(2):
            q = 2 * (1 - zl) + j
            slabs = [((1 - zl) * g + zl * r, 16 * q + (1 - zl) * r + zl * g) for r in range(16)]
            ints_rows(slabs, pl.multiple_of(256 * j + 16 * g, 16))
        return 0

    lax.fori_loop(0, 16, cross, 0, unroll=2)

    def diagonal(g, _):
        turn = [(r + g + 1) % 16 for r in range(16)]
        ints_rows([(r, 16 * pair + turn[r]) for r in range(16)], pl.multiple_of(512 + 16 * g, 16))
        ints_rows([(turn[r], 16 * pair + r) for r in range(16)], pl.multiple_of(768 + 16 * g, 16))
        half = g // 4
        vh = (half + c) % 2
        slabs = [(8 * half + 2 * (g % 4) + r // 8, 16 * pn + 8 * vh + r % 8) for r in range(16)]
        ints_rows(slabs, pl.multiple_of(640 + 16 * g, 16))
        return 0

    lax.fori_loop(0, 8, diagonal, 0, unroll=2)
    for cp in icopies:
        cp.wait_recv()

    def minus(g, _):
        half = (g // 4 + c) % 2
        slabs = [rcore[half, r % 8, pl.ds(2 * (g % 4) + r // 8, 1)] for r in range(16)]
        store_group(jnp.concatenate(slabs, axis=0), flat_i, pl.multiple_of(896 + 16 * g, 16))
        return 0

    lax.fori_loop(0, 8, minus, 0, unroll=4)
    core_amps.wait_recv()

    def early_rows(n, _):
        amps_rows(0, 1, n // 4, n % 4, pl.multiple_of(16 * n, 16))
        return 0

    lax.fori_loop(0, 16, early_rows, 0, unroll=4)

    def ladder(row0, rows, turned=False):
        a = flat_a[row0 : row0 + rows, :]
        def columns(first):
            if turned:
                return jnp.dot(a, flat_t[:, first : first + 256], preferred_element_type=jnp.float32)
            return lax.dot_general(a, flat_i[first : first + 256, :], NT_DIMS, preferred_element_type=jnp.float32)

        for n in range(2):
            part[row0 : row0 + rows, 256 * n : 256 * (n + 1)] = columns(256 * n)
        part[row0 : row0 + rows, 512:768] = columns(512) - columns(768)

    def xcopy(s, j):
        to = (x + j) % 4
        return remote(
            xsend.at[s, to], xrecv.at[s, j - 1], xss.at[s, j - 1], xrs.at[s, j - 1], dev(x_=to)
        )

    def send_x(s):
        packed = pack(part[64 * s : 64 * s + 64, :])
        for xq in range(4):
            xsend[s, xq] = packed[16 * xq : 16 * xq + 16]
        for j in (2, 1, 3):
            xcopy(s, j).start()

    def ydest(s, slot):
        k = s % 4
        zsrc = zl if s < 4 else 1 - zl
        p = 2 * zsrc + (c if slot == 0 else 1 - c)
        to = 2 * p + k // 2
        return to, (y - to + 8) % 8, k % 2

    def ycopy(s, slot):
        to, j, h = ydest(s, slot)
        return remote(ysend.at[s, slot], yrecv.at[h, j], yss.at[s, slot], yrs.at[h, j], dev(y_=to))

    def reduce_x(s):
        for j in (1, 3, 2):
            xcopy(s, j).wait_recv()
        total = part[pl.ds(pl.multiple_of(64 * s + 16 * x, 16), 16), :]
        for j in (1, 3, 2):
            total = total + unpack(xrecv[s, j - 1])
        packed = pack(total)
        for slot in range(2):
            ysend[s, slot] = packed[8 * slot : 8 * slot + 8]
            _, j, h = ydest(s, slot)

            @pl.when(j != 0)
            def _():
                ycopy(s, slot).start()

            @pl.when(j == 0)
            def _():
                yown[h] = total[8 * slot : 8 * slot + 8]

    ladder(0, 256)
    for s in range(4):
        send_x(s)

    def build_place():
        col = lax.broadcasted_iota(jnp.int32, (1, 1024), 1)
        u, b = col // 64, col % 64
        block, v = b // 16, b % 16
        turn = (v - u + 16) % 16
        diag_plus = jnp.logical_or(turn < 8, jnp.logical_and(turn == 8, u < 8))
        src = jnp.where(diag_plus, 512 + (turn - 1) * 16 + u, 512 + (15 - turn) * 16 + v)
        sign = jnp.where(diag_plus, 1.0, -1.0)
        src = jnp.where(turn == 0, -1, src)
        uh, vh, u8, v8 = u // 8, v // 8, u % 8, v % 8
        mine = (uh + vh) % 2 == c
        near = block == pn
        src = jnp.where(near, jnp.where(mine, 640 + uh * 64 + u8 * 8 + v8, 768 + vh * 64 + v8 * 8 + u8), src)
        sign = jnp.where(near, jnp.where(mine, 1.0, -1.0), sign)
        far = block // 2 == 1 - zl
        src = jnp.where(far, (block % 2) * 256 + (1 - zl) * (u * 16 + v) + zl * (v * 16 + u), src)
        sign = jnp.where(far, 1.0, sign)

        def body(r, _):
            rows = r * 64 + lax.broadcasted_iota(jnp.int32, (64, 1024), 0)
            picked = jnp.where(rows == src, sign, 0.0)
            place[pl.ds(pl.multiple_of(r * 64, 64), 64), :] = picked.astype(jnp.bfloat16)
            return 0

        lax.fori_loop(0, 14, body, 0)

    def turn_ints(n, _):
        rows, cols = pl.multiple_of(n % 4 * 256, 256), pl.multiple_of(n // 4 * 256, 256)
        flat_t[pl.ds(cols, 256), pl.ds(rows, 256)] = flat_i[pl.ds(rows, 256), pl.ds(cols, 256)].T
        return 0

    lax.fori_loop(0, 32, turn_ints, 0, unroll=2)

    fwds = []
    for k in range(4):
        s = 4 + k
        for n in (2 * k, 2 * k + 1):
            zcopies[n].wait_recv()
            at = pl.ds(first_row(k, n % 2), 16)
            fwd = remote(raw.at[2, at], raw.at[3, at], asend.at[9 + n], arecv.at[9 + n], core_dev)
            fwd.start()
            fwds.append(fwd)
        if k == 1:
            reduce_x(0)
        if k == 2:
            reduce_x(1)
        if k == 3:
            reduce_x(2)
            reduce_x(3)
        for fwd in fwds[2 * k :]:
            fwd.wait_recv()

        def late_rows(n, _):
            amps_rows(2, 3, k, n, pl.multiple_of(64 * s + 16 * n, 16))
            return 0

        lax.fori_loop(0, 4, late_rows, 0, unroll=4)
        ladder(64 * s, 64, True)
        send_x(s)
    for s in range(4, 8):
        reduce_x(s)
    build_place()

    def zcopies_of(to, n):
        jz = (to - zh + 4) % 4
        far = [
            remote(
                zs.at[to, :, pl.ds(256 * j, 256)], zq.at[c, jz], zss.at[n, j], zrs.at[jz, c],
                dev(zh_=to, pair_=2 * (1 - zl) + j),
            )
            for j in range(2)
        ]
        near = remote(
            zs.at[to, :, pl.ds(640, 128)], znbr.at[jz], zss.at[n, 3], zrs.at[jz, 3], dev(zh_=to, pair_=pn)
        )
        return jz, far + [near], remote(zs.at[to], zsame.at[jz], zss.at[n, 2], zrs.at[jz, 2], dev(zh_=to))

    for h in range(2):
        total = yown[h]
        for j in range(1, 8):
            remote(ysend.at[0, 0], yrecv.at[h, j], yss.at[0, 0], yrs.at[h, j], core_dev).wait_recv()
        for j in range(1, 8):
            total = total + unpack(yrecv[h, j])
        for zb in range(2):
            zs[2 * zb + h] = total[4 * zb : 4 * zb + 4]
        for zb in range(2):
            jz, copies, same_copy = zcopies_of(2 * zb + h, 2 * zb + h)

            @pl.when(jz != 0)
            def _():
                same_copy.start()

            for cp in copies:
                cp.start()

    for cp in sends + fwds:
        cp.wait_send()
    for s in range(8):
        for j in range(1, 4):
            xcopy(s, j).wait_send()
        for slot in range(2):
            @pl.when(ydest(s, slot)[1] != 0)
            def _():
                ycopy(s, slot).wait_send()

    same = zs[zh]
    for jz in range(1, 4):
        remote(zs.at[0], zsame.at[jz], zss.at[jz, 2], zrs.at[jz, 2], core_dev).wait_recv()
        same = same + zsame[jz]
    near = None
    for jz in range(4):
        remote(zs.at[0, :, pl.ds(0, 128)], znbr.at[jz], zss.at[jz, 3], zrs.at[jz, 3], core_dev).wait_recv()
        near = znbr[jz] if near is None else near + znbr[jz]
    far = []
    for j in range(2):
        got = None
        for jz in range(4):
            remote(zs.at[0, :, pl.ds(0, 256)], zq.at[j, jz], zss.at[jz, j], zrs.at[jz, j], core_dev).wait_recv()
            got = zq[j, jz] if got is None else got + zq[j, jz]
        far.append(got)
    values = jnp.concatenate(
        [same[:, 0:256] - far[0], same[:, 256:512] - far[1], same[:, 512:768], near], axis=1
    )
    values = (0.5 * values).astype(jnp.bfloat16)
    out[...] = jnp.dot(values, place[...], preferred_element_type=jnp.float32).astype(jnp.bfloat16)
    for n in range(4):
        jz, copies, same_copy = zcopies_of(n, n)
        for cp in copies:
            cp.wait_send()

        @pl.when(jz != 0)
        def _():
            same_copy.wait_send()


def per_device(amps, integrals, mask_amps, mask_ints):
    ints = integrals.reshape(16, 64, 16, 128)
    bf, f32 = jnp.bfloat16, jnp.float32
    dma = pltpu.SemaphoreType.DMA
    return pl.pallas_call(
        kernel,
        out_shape=jax.ShapeDtypeStruct((4, 1024), bf),
        in_specs=[pl.BlockSpec(memory_space=pltpu.HBM)] * 4,
        out_specs=pl.BlockSpec(memory_space=pltpu.VMEM),
        scratch_shapes=[
            pltpu.SMEM((8, 8), jnp.int32),
            pltpu.SMEM((8, 8), jnp.int32),
            pltpu.VMEM((4, 128, 16, 128), bf),
            pltpu.VMEM((16, 64, 16, 128), bf),
            pltpu.VMEM((2, 8, 8, 16, 128), bf),
            pltpu.VMEM((512, 2048), bf),
            pltpu.VMEM((1024, 2048), bf),
            pltpu.VMEM((2048, 1024), bf),
            pltpu.VMEM((512, COLS), f32),
            pltpu.VMEM((8, 4, 16, PACKED), f32),
            pltpu.VMEM((8, 3, 16, PACKED), f32),
            pltpu.VMEM((8, 2, 8, PACKED), f32),
            pltpu.VMEM((2, 8, 8, PACKED), f32),
            pltpu.VMEM((2, 8, COLS), f32),
            pltpu.VMEM((4, 4, COLS), f32),
            pltpu.VMEM((4, 4, COLS), f32),
            pltpu.VMEM((4, 4, 128), f32),
            pltpu.VMEM((2, 4, 4, 256), f32),
            pltpu.VMEM((896, 1024), bf),
            dma((4,)), dma((17,)), dma((17,)), dma((2,)), dma((2,)),
            dma((8, 3)), dma((8, 3)), dma((8, 2)), dma((2, 8)), dma((4, 4)), dma((4, 4)),
        ],
        compiler_params=pltpu.CompilerParams(
            collective_id=0, has_side_effects=True, vmem_limit_bytes=61 * 2**20
        ),
        cost_estimate=pl.CostEstimate(flops=2 * 512 * 1024 * 2048, bytes_accessed=5 * 2**20, transcendentals=0),
    )(amps, ints, mask_amps, mask_ints)


def solution(mesh):
    return jax.shard_map(
        per_device,
        mesh=mesh,
        in_specs=(P("pair", "row", "col"), P("pair", "row", "col"), P(), P()),
        out_specs=P(("row", "col"), "pair"),
        check_vma=False,
    )
```

```python
import functools

import jax
import jax.numpy as jnp
from jax import lax
from jax.experimental import pallas as pl
from jax.experimental.pallas import tpu as pltpu
from jax.sharding import PartitionSpec as P

MESH = pl.DeviceIdType.MESH
NT_DIMS = (((1,), (1,)), ((), ()))
COLS = 768
PACKED = 512


def pack(v):
    top = jnp.maximum(jnp.max(jnp.abs(v), axis=1, keepdims=True), 1e-30)
    power = jnp.floor(jnp.log2(top)) + 1.0
    q = jnp.round(v * (jnp.exp2(15.0 - power) * 0.9999))
    q1, q2, q3 = q[:, 0:256], q[:, 256:512], q[:, 512:768]
    lane = lax.broadcasted_iota(jnp.int32, q3.shape, 1)
    q3 = jnp.where(lane == 120, power, q3)
    high = jnp.round(q3 * (1.0 / 256.0))
    low = q3 - 256.0 * high
    return jnp.concatenate([q1 * 512.0 + high, q2 * 512.0 + low], axis=1)


def unpack(w):
    w1, w2 = w[:, 0:256], w[:, 256:512]
    q1 = jnp.round(w1 * (1.0 / 512.0))
    q2 = jnp.round(w2 * (1.0 / 512.0))
    q3 = 256.0 * (w1 - 512.0 * q1) + (w2 - 512.0 * q2)
    power = q3[:, 120:121]
    scale = jnp.exp2(power - 15.0) * (1.0 / 0.9999)
    return jnp.concatenate([q1, q2, q3], axis=1) * scale


def store_group(slabs, dst, row):
    turned = jnp.swapaxes(slabs, 0, 1)
    for c in range(16):
        dst[pl.ds(row, 16), c * 128 : (c + 1) * 128] = turned[c]


def kernel(
    amps, ints, mask_a_hbm, mask_i_hbm, out,
    mask_a, mask_i, raw, ints_v, rcore, flat_a, flat_i, flat_t, part, xsend, xrecv, ysend, yrecv, yown,
    zs, zsame, znbr, zq, place,
    lsem, asend, arecv, isend, irecv, xss, xrs, yss, yrs, zss, zrs,
):
    row, x, pair = lax.axis_index("row"), lax.axis_index("col"), lax.axis_index("pair")
    y, zh = row // 4, row % 4
    zl, c = pair // 2, pair % 2
    pn = 2 * zl + 1 - c

    def dev(y_=None, zh_=None, x_=None, pair_=None):
        yy = y if y_ is None else y_
        zz = zh if zh_ is None else zh_
        return {
            "row": yy * 4 + zz,
            "col": x if x_ is None else x_,
            "pair": pair if pair_ is None else pair_,
        }

    core_dev = dev(pair_=pn)
    zl_dev = dev(pair_=2 * (1 - zl) + c)

    def first_row(k, zb):
        return 64 * (k // 2) + 32 * zb + 16 * (k % 2)

    def remote(src, dst, ss, rs, device):
        return pltpu.make_async_remote_copy(src, dst, ss, rs, device_id=device, device_id_type=MESH)

    barrier = pltpu.get_barrier_semaphore()
    peers = [dev(x_=(x + j) % 4) for j in range(1, 4)]
    peers += [dev(y_=(y + j) % 8) for j in range(1, 8)]
    peers += [
        dev(zh_=(zh + jz) % 4, pair_=(pair + jp) % 4) for jz in range(4) for jp in range(4) if jz or jp
    ]
    for device in peers:
        pl.semaphore_signal(barrier, inc=1, device_id=device, device_id_type=MESH)

    own_copy = pltpu.make_async_copy(amps, raw.at[0], lsem.at[0])
    own_copy.start()
    ints_copy = pltpu.make_async_copy(ints, ints_v, lsem.at[1])
    ints_copy.start()
    mask_copies = [
        pltpu.make_async_copy(mask_a_hbm, mask_a, lsem.at[2]),
        pltpu.make_async_copy(mask_i_hbm, mask_i, lsem.at[3]),
    ]
    for cp in mask_copies:
        cp.start()
    pl.semaphore_wait(barrier, len(peers))

    sends = []
    core_amps = remote(amps, raw.at[1], asend.at[0], arecv.at[0], core_dev)
    core_amps.start()
    sends.append(core_amps)
    zcopies = []
    for n in range(8):
        at = pl.ds(first_row(n // 2, n % 2), 16)
        cp = remote(amps.at[at], raw.at[2, at], asend.at[1 + n], arecv.at[1 + n], zl_dev)
        cp.start()
        zcopies.append(cp)
        sends.append(cp)
    icopies = []
    for a in range(2):
        vh = (a + 1 + c) % 2
        cp = remote(
            ints.at[pl.ds(8 * a, 8), pl.ds(16 * pn + 8 * vh, 8)], rcore.at[a], isend.at[a], irecv.at[a], core_dev
        )
        cp.start()
        icopies.append(cp)
        sends.append(cp)

    for cp in mask_copies:
        cp.wait()
    m0 = (mask_a[y, 2 * x] * mask_i[y, 2 * x]).astype(jnp.float32)
    m1 = (mask_a[y, 2 * x + 1] * mask_i[y, 2 * x + 1]).astype(jnp.float32)
    lane = lax.broadcasted_iota(jnp.int32, (16, 128), 1)
    factor = jnp.where(lane < 64, m0, m1).astype(jnp.bfloat16)

    def amps_rows(first, second, k, xq, dst_row):
        parts = [
            raw[src, pl.ds(first_row(k, zb) + 4 * xq, 4)] for src in (first, second) for zb in range(2)
        ]
        store_group(jnp.concatenate(parts, axis=0) * factor[None], flat_a, dst_row)

    def ints_rows(slabs, dst_row):
        store_group(jnp.concatenate([ints_v[a, pl.ds(b, 1)] for a, b in slabs], axis=0), flat_i, dst_row)

    own_copy.wait()
    ints_copy.wait()

    def cross(g, _):
        for j in range(2):
            q = 2 * (1 - zl) + j
            slabs = [((1 - zl) * g + zl * r, 16 * q + (1 - zl) * r + zl * g) for r in range(16)]
            ints_rows(slabs, pl.multiple_of(256 * j + 16 * g, 16))
        return 0

    lax.fori_loop(0, 16, cross, 0, unroll=4)

    def diagonal(g, _):
        turn = [(r + g + 1) % 16 for r in range(16)]
        ints_rows([(r, 16 * pair + turn[r]) for r in range(16)], pl.multiple_of(512 + 16 * g, 16))
        ints_rows([(turn[r], 16 * pair + r) for r in range(16)], pl.multiple_of(768 + 16 * g, 16))
        half = g // 4
        vh = (half + c) % 2
        slabs = [(8 * half + 2 * (g % 4) + r // 8, 16 * pn + 8 * vh + r % 8) for r in range(16)]
        ints_rows(slabs, pl.multiple_of(640 + 16 * g, 16))
        return 0

    lax.fori_loop(0, 8, diagonal, 0, unroll=4)
    for cp in icopies:
        cp.wait_recv()

    def minus(g, _):
        half = (g // 4 + c) % 2
        slabs = [rcore[half, r % 8, pl.ds(2 * (g % 4) + r // 8, 1)] for r in range(16)]
        store_group(jnp.concatenate(slabs, axis=0), flat_i, pl.multiple_of(896 + 16 * g, 16))
        return 0

    lax.fori_loop(0, 8, minus, 0, unroll=4)
    core_amps.wait_recv()

    def early_rows(n, _):
        amps_rows(0, 1, n // 4, n % 4, pl.multiple_of(16 * n, 16))
        return 0

    lax.fori_loop(0, 16, early_rows, 0, unroll=8)

    def ladder(row0, rows, turned=False):
        a = flat_a[row0 : row0 + rows, :]
        def columns(first):
            if turned:
                return jnp.dot(a, flat_t[:, first : first + 256], preferred_element_type=jnp.float32)
            return lax.dot_general(a, flat_i[first : first + 256, :], NT_DIMS, preferred_element_type=jnp.float32)

        for n in range(2):
            part[row0 : row0 + rows, 256 * n : 256 * (n + 1)] = columns(256 * n)
        part[row0 : row0 + rows, 512:768] = columns(512) - columns(768)

    def xcopy(s, j):
        to = (x + j) % 4
        return remote(
            xsend.at[s, to], xrecv.at[s, j - 1], xss.at[s, j - 1], xrs.at[s, j - 1], dev(x_=to)
        )

    def send_x(s):
        packed = pack(part[64 * s : 64 * s + 64, :])
        for xq in range(4):
            xsend[s, xq] = packed[16 * xq : 16 * xq + 16]
        for j in (2, 1, 3):
            xcopy(s, j).start()

    def ydest(s, slot):
        k = s % 4
        zsrc = zl if s < 4 else 1 - zl
        p = 2 * zsrc + (c if slot == 0 else 1 - c)
        to = 2 * p + k // 2
        return to, (y - to + 8) % 8, k % 2

    def ycopy(s, slot):
        to, j, h = ydest(s, slot)
        return remote(ysend.at[s, slot], yrecv.at[h, j], yss.at[s, slot], yrs.at[h, j], dev(y_=to))

    def reduce_x(s):
        for j in (1, 3, 2):
            xcopy(s, j).wait_recv()
        total = part[pl.ds(pl.multiple_of(64 * s + 16 * x, 16), 16), :]
        for j in (1, 3, 2):
            total = total + unpack(xrecv[s, j - 1])
        packed = pack(total)
        for slot in range(2):
            ysend[s, slot] = packed[8 * slot : 8 * slot + 8]
            _, j, h = ydest(s, slot)

            @pl.when(j != 0)
            def _():
                ycopy(s, slot).start()

            @pl.when(j == 0)
            def _():
                yown[h] = total[8 * slot : 8 * slot + 8]

    ladder(0, 256)
    for s in range(4):
        send_x(s)

    def build_place():
        col = lax.broadcasted_iota(jnp.int32, (1, 1024), 1)
        u, b = col // 64, col % 64
        block, v = b // 16, b % 16
        turn = (v - u + 16) % 16
        diag_plus = jnp.logical_or(turn < 8, jnp.logical_and(turn == 8, u < 8))
        src = jnp.where(diag_plus, 512 + (turn - 1) * 16 + u, 512 + (15 - turn) * 16 + v)
        sign = jnp.where(diag_plus, 1.0, -1.0)
        src = jnp.where(turn == 0, -1, src)
        uh, vh, u8, v8 = u // 8, v // 8, u % 8, v % 8
        mine = (uh + vh) % 2 == c
        near = block == pn
        src = jnp.where(near, jnp.where(mine, 640 + uh * 64 + u8 * 8 + v8, 768 + vh * 64 + v8 * 8 + u8), src)
        sign = jnp.where(near, jnp.where(mine, 1.0, -1.0), sign)
        far = block // 2 == 1 - zl
        src = jnp.where(far, (block % 2) * 256 + (1 - zl) * (u * 16 + v) + zl * (v * 16 + u), src)
        sign = jnp.where(far, 1.0, sign)

        def body(r, _):
            rows = r * 64 + lax.broadcasted_iota(jnp.int32, (64, 1024), 0)
            picked = jnp.where(rows == src, sign, 0.0)
            place[pl.ds(pl.multiple_of(r * 64, 64), 64), :] = picked.astype(jnp.bfloat16)
            return 0

        lax.fori_loop(0, 14, body, 0)

    def turn_ints(n, _):
        rows, cols = pl.multiple_of(n % 4 * 256, 256), pl.multiple_of(n // 4 * 256, 256)
        flat_t[pl.ds(cols, 256), pl.ds(rows, 256)] = flat_i[pl.ds(rows, 256), pl.ds(cols, 256)].T
        return 0

    lax.fori_loop(0, 32, turn_ints, 0, unroll=4)

    fwds = []
    for k in range(4):
        s = 4 + k
        for n in (2 * k, 2 * k + 1):
            zcopies[n].wait_recv()
            at = pl.ds(first_row(k, n % 2), 16)
            fwd = remote(raw.at[2, at], raw.at[3, at], asend.at[9 + n], arecv.at[9 + n], core_dev)
            fwd.start()
            fwds.append(fwd)
        if k == 1:
            reduce_x(0)
        if k == 2:
            reduce_x(1)
        if k == 3:
            reduce_x(2)
            reduce_x(3)
        for fwd in fwds[2 * k :]:
            fwd.wait_recv()

        def late_rows(n, _):
            amps_rows(2, 3, k, n, pl.multiple_of(64 * s + 16 * n, 16))
            return 0

        lax.fori_loop(0, 4, late_rows, 0, unroll=4)
        ladder(64 * s, 64, True)
        send_x(s)
    for s in range(4, 8):
        reduce_x(s)
    build_place()

    def zcopies_of(to, n):
        jz = (to - zh + 4) % 4
        far = [
            remote(
                zs.at[to, :, pl.ds(256 * j, 256)], zq.at[c, jz], zss.at[n, j], zrs.at[jz, c],
                dev(zh_=to, pair_=2 * (1 - zl) + j),
            )
            for j in range(2)
        ]
        near = remote(
            zs.at[to, :, pl.ds(640, 128)], znbr.at[jz], zss.at[n, 3], zrs.at[jz, 3], dev(zh_=to, pair_=pn)
        )
        return jz, far + [near], remote(zs.at[to], zsame.at[jz], zss.at[n, 2], zrs.at[jz, 2], dev(zh_=to))

    for h in range(2):
        total = yown[h]
        for j in range(1, 8):
            remote(ysend.at[0, 0], yrecv.at[h, j], yss.at[0, 0], yrs.at[h, j], core_dev).wait_recv()
        for j in range(1, 8):
            total = total + unpack(yrecv[h, j])
        for zb in range(2):
            zs[2 * zb + h] = total[4 * zb : 4 * zb + 4]
        for zb in range(2):
            jz, copies, same_copy = zcopies_of(2 * zb + h, 2 * zb + h)

            @pl.when(jz != 0)
            def _():
                same_copy.start()

            for cp in copies:
                cp.start()

    for cp in sends + fwds:
        cp.wait_send()
    for s in range(8):
        for j in range(1, 4):
            xcopy(s, j).wait_send()
        for slot in range(2):
            @pl.when(ydest(s, slot)[1] != 0)
            def _():
                ycopy(s, slot).wait_send()

    same = zs[zh]
    for jz in range(1, 4):
        remote(zs.at[0], zsame.at[jz], zss.at[jz, 2], zrs.at[jz, 2], core_dev).wait_recv()
        same = same + zsame[jz]
    near = None
    for jz in range(4):
        remote(zs.at[0, :, pl.ds(0, 128)], znbr.at[jz], zss.at[jz, 3], zrs.at[jz, 3], core_dev).wait_recv()
        near = znbr[jz] if near is None else near + znbr[jz]
    far = []
    for j in range(2):
        got = None
        for jz in range(4):
            remote(zs.at[0, :, pl.ds(0, 256)], zq.at[j, jz], zss.at[jz, j], zrs.at[jz, j], core_dev).wait_recv()
            got = zq[j, jz] if got is None else got + zq[j, jz]
        far.append(got)
    values = jnp.concatenate(
        [same[:, 0:256] - far[0], same[:, 256:512] - far[1], same[:, 512:768], near], axis=1
    )
    values = (0.5 * values).astype(jnp.bfloat16)
    out[...] = jnp.dot(values, place[...], preferred_element_type=jnp.float32).astype(jnp.bfloat16)
    for n in range(4):
        jz, copies, same_copy = zcopies_of(n, n)
        for cp in copies:
            cp.wait_send()

        @pl.when(jz != 0)
        def _():
            same_copy.wait_send()


def per_device(amps, integrals, mask_amps, mask_ints):
    ints = integrals.reshape(16, 64, 16, 128)
    bf, f32 = jnp.bfloat16, jnp.float32
    dma = pltpu.SemaphoreType.DMA
    return pl.pallas_call(
        kernel,
        out_shape=jax.ShapeDtypeStruct((4, 1024), bf),
        in_specs=[pl.BlockSpec(memory_space=pltpu.HBM)] * 4,
        out_specs=pl.BlockSpec(memory_space=pltpu.VMEM),
        scratch_shapes=[
            pltpu.SMEM((8, 8), jnp.int32),
            pltpu.SMEM((8, 8), jnp.int32),
            pltpu.VMEM((4, 128, 16, 128), bf),
            pltpu.VMEM((16, 64, 16, 128), bf),
            pltpu.VMEM((2, 8, 8, 16, 128), bf),
            pltpu.VMEM((512, 2048), bf),
            pltpu.VMEM((1024, 2048), bf),
            pltpu.VMEM((2048, 1024), bf),
            pltpu.VMEM((512, COLS), f32),
            pltpu.VMEM((8, 4, 16, PACKED), f32),
            pltpu.VMEM((8, 3, 16, PACKED), f32),
            pltpu.VMEM((8, 2, 8, PACKED), f32),
            pltpu.VMEM((2, 8, 8, PACKED), f32),
            pltpu.VMEM((2, 8, COLS), f32),
            pltpu.VMEM((4, 4, COLS), f32),
            pltpu.VMEM((4, 4, COLS), f32),
            pltpu.VMEM((4, 4, 128), f32),
            pltpu.VMEM((2, 4, 4, 256), f32),
            pltpu.VMEM((896, 1024), bf),
            dma((4,)), dma((17,)), dma((17,)), dma((2,)), dma((2,)),
            dma((8, 3)), dma((8, 3)), dma((8, 2)), dma((2, 8)), dma((4, 4)), dma((4, 4)),
        ],
        compiler_params=pltpu.CompilerParams(
            collective_id=0, has_side_effects=True, vmem_limit_bytes=61 * 2**20
        ),
        cost_estimate=pl.CostEstimate(flops=2 * 512 * 1024 * 2048, bytes_accessed=5 * 2**20, transcendentals=0),
    )(amps, ints, mask_amps, mask_ints)


def solution(mesh):
    return jax.shard_map(
        per_device,
        mesh=mesh,
        in_specs=(P("pair", "row", "col"), P("pair", "row", "col"), P(), P()),
        out_specs=P(("row", "col"), "pair"),
        check_vma=False,
    )
```
